32 devices in a mesh: site: 4 (over x, core), sec: 8 (over z, y).
Axes of the slice: x: 2, y: 2, z: 4, core: 2. Of those that a mesh axis runs over, the one named last changes fastest.
Arguments:
- tensors: bfloat16 [4, 16, 4, 512, 512], P('site', 'sec'), as said below
- factors: float32 [4, 16, 512, 512], P('site', 'sec'), as said below
- sector_sizes: int32 [4, 16], replicated, may hold values from 384 to 512, as said below
- merging: int32 [4, 16, 4], replicated, may hold values from 0 to 15, as said below
Outputs:
- isometry: float32 [4, 16, 4, 512, 512], P('site', 'sec')
- factor_out: float32 [4, 16, 512, 512], P('site', 'sec')
The draws below stay inside these ranges and needn't reach their ends.
Inputs may be any that keep to these rules, and one draw needn't show every extreme that they name: `sector_sizes`: every bond has one sector of exactly 512 states and one of exactly 384. For every site and physical state, merging maps the left sectors one to one onto the right sectors; the 8 blocks (left sector, physical state) of the left sectors that lie on one index of sec go to 8 different indices of sec, one block to each. `tensors`: zero outside the rows below the left sector's size and the columns below the right sector's size. `factors`: upper triangular with a positive diagonal inside the sector's size, the identity on its padding.
All inputs are finite; a program needn't handle non-finite values.
Results may differ from the reference program's by a relative error of at most 0.007.
Values may be sent and summed in bfloat16 or wider, within the bound.
A program may use at most 192 MiB of HBM per device.

```python
import math
import jax
import jax.numpy as jnp
from jax import lax

BLK = 512
PHYS = 4
SEC_DEV = 2
ROUNDS = 3
NSEC = 16
SITES = 4


def sector_widths(key):
    key_base, key_first, key_second = jax.random.split(jax.random.fold_in(key, 101), 3)
    drawn_widths = jax.random.randint(key_base, (SITES, NSEC), 3 * BLK // 4, BLK + 1)
    first_pos = jax.random.randint(key_first, (SITES,), 0, NSEC)
    second_pos = (first_pos + 1 + jax.random.randint(key_second, (SITES,), 0, NSEC - 1)) % NSEC
    columns = jnp.arange(NSEC, dtype=jnp.int32)[None, :]
    drawn_widths = jnp.where(columns == first_pos[:, None], BLK, drawn_widths)
    drawn_widths = jnp.where(columns == second_pos[:, None], 3 * BLK // 4, drawn_widths)
    return drawn_widths.astype(jnp.int32)


def one_site_table(site_key):
    groups = NSEC // SEC_DEV
    key_first, key_second, key_offset, key_turn = jax.random.split(site_key, 4)
    first_perm = jax.random.permutation(key_first, groups)
    second_perm = jax.random.permutation(key_second, groups)
    offsets = jax.random.permutation(key_offset, groups)[:SEC_DEV * PHYS]
    turned = jax.random.randint(key_turn, (PHYS, groups), 0, SEC_DEV)
    columns_out = []
    for phys_index in range(PHYS):
        inner_cols = []
        for inner in range(SEC_DEV):
            dest_dev = second_perm[(first_perm + offsets[inner * PHYS + phys_index]) % groups]
            turn_here = turned[phys_index][dest_dev]
            inner_cols.append(dest_dev * SEC_DEV + (inner + turn_here) % SEC_DEV)
        columns_out.append(jnp.stack(inner_cols, axis=1).reshape(NSEC))
    return jnp.stack(columns_out, axis=-1).astype(jnp.int32)


def merging_table(key):
    site_keys = jax.random.split(jax.random.fold_in(key, 202), SITES)
    return jax.vmap(one_site_table)(site_keys)


def draw_sector_sizes(key, part):
    return sector_widths(key)


def draw_merging(key, part):
    return merging_table(key)


def draw_tensors(key, part):
    widths = sector_widths(key)
    table = merging_table(key)
    key_values = jax.random.fold_in(jax.random.fold_in(key, 303), 0)
    spread_scale = (PHYS * BLK) ** (-0.5)
    full_shape = (SITES, NSEC, PHYS, BLK, BLK)
    values_drawn = jax.random.normal(key_values, full_shape, jnp.float32) * spread_scale
    next_widths = jnp.roll(widths, -1, axis=0)
    selector = (table[..., None] == jnp.arange(NSEC, dtype=jnp.int32)).astype(jnp.int32)
    column_widths = jnp.sum(selector * next_widths[:, None, None, :], axis=-1)
    positions = jnp.arange(BLK, dtype=jnp.int32)
    rows_inside = positions[None, None, None, :, None] < widths[:, :, None, None, None]
    columns_inside = positions[None, None, None, None, :] < column_widths[:, :, :, None, None]
    return jnp.where(rows_inside & columns_inside, values_drawn, 0.0).astype(jnp.bfloat16)


def draw_factors(key, part):
    widths = sector_widths(key)
    key_diag, key_upper = jax.random.split(jax.random.fold_in(key, 404))
    full_shape = (SITES, NSEC, BLK, BLK)
    diagonal = jnp.exp(jax.random.uniform(key_diag, (SITES, NSEC, BLK, 1), jnp.float32, math.log(0.5), math.log(2.0)))
    upper_vals = jax.random.normal(key_upper, full_shape, jnp.float32) * (0.5 / math.sqrt(BLK))
    positions = jnp.arange(BLK, dtype=jnp.int32)
    row_inside = positions[None, None, :, None] < widths[:, :, None, None]
    column_inside = positions[None, None, None, :] < widths[:, :, None, None]
    on_diagonal = positions[:, None] == positions[None, :]
    above = positions[:, None] < positions[None, :]
    inside = row_inside & column_inside
    result = jnp.where(on_diagonal[None, None] & inside, diagonal, 0.0)
    result = jnp.where(above[None, None] & inside, upper_vals, result)
    result = jnp.where(on_diagonal[None, None] & jnp.logical_not(inside), 1.0, result)
    return result.astype(jnp.float32)


def setup_inputs(seed: int = 0) -> dict:
    key_list = jax.random.split(jax.random.key(seed), 5)
    return {
        "tensors": draw_tensors(jax.random.fold_in(key_list[4], 71), 0),
        "factors": draw_factors(jax.random.fold_in(key_list[4], 71), 0),
        "sector_sizes": draw_sector_sizes(jax.random.fold_in(key_list[4], 71), 0),
        "merging": draw_merging(jax.random.fold_in(key_list[4], 71), 0),
    }


HIGH = lax.Precision.HIGHEST

def stack_site(inputs):
    blocks, carried, merging_rows, widths = inputs
    left_factor = carried.astype(jnp.bfloat16).astype(jnp.float32)
    products = jnp.einsum('ajk,apkl->apjl', left_factor, blocks.astype(jnp.float32), precision=HIGH).astype(jnp.bfloat16)
    selector = (merging_rows[:, :, None] == jnp.arange(NSEC, dtype=jnp.int32)[None, None, :]).astype(jnp.float32)
    stacked = jnp.einsum('apb,apjl->bpjl', selector, products.astype(jnp.float32), precision=HIGH)
    stacked = stacked.reshape(NSEC, PHYS * BLK, BLK)
    gram_matrix = jnp.einsum('brl,brm->blm', stacked, stacked, precision=HIGH)
    padding = (jnp.arange(BLK, dtype=jnp.int32)[None, :] >= widths[:, None]).astype(jnp.float32)
    gram_matrix = gram_matrix + jnp.eye(BLK, dtype=jnp.float32)[None] * padding[:, None, :]
    lower_factor = jnp.linalg.cholesky(gram_matrix)
    return (lower_factor, stacked)

def factor_site(inputs):
    lower_factor, stacked = stack_site(inputs)
    return jnp.swapaxes(lower_factor, -1, -2)

def final_site(inputs):
    lower_factor, stacked = stack_site(inputs)
    solved = lax.linalg.triangular_solve(lower_factor, stacked, left_side=False, lower=True, transpose_a=True)
    scaled = (solved * math.sqrt(PHYS * BLK)).reshape(NSEC, PHYS, BLK, BLK)
    return (jnp.swapaxes(lower_factor, -1, -2), scaled)

def reference(tensors, factors, sector_sizes, merging):
    widths = jnp.roll(sector_sizes, -1, axis=0)
    carried = factors
    for step_index in range(ROUNDS - 1):
        upper_factor = lax.map(factor_site, (tensors, carried, merging, widths))
        carried = jnp.roll(upper_factor, 1, axis=0)
    upper_out, isometry = lax.map(final_site, (tensors, carried, merging, widths))
    return (isometry, upper_out)
```

```python
import functools
import math

import jax
import jax.numpy as jnp
from jax import lax
from jax.experimental import pallas as pl
from jax.experimental.pallas import tpu as pltpu
from jax.sharding import PartitionSpec as P

ROUNDS = 3
TILE = 128
SUB = 8
HIGH = lax.Precision.HIGHEST


def from_behind(shard, axis, by):
    size = lax.axis_size(axis)
    return lax.ppermute(shard, axis, [(i, (i + by) % size) for i in range(size)])


def products_kernel(target_ref, factor_ref, block_ref, out_ref):
    out_ref[0] = jnp.dot(
        factor_ref[0].astype(jnp.bfloat16), block_ref[0], preferred_element_type=jnp.float32
    ).astype(jnp.bfloat16)


def products_by_target(factor, blocks, target, groups):
    count, size = blocks.shape[0], blocks.shape[-1]
    phys_count = count // factor.shape[0]
    return pl.pallas_call(
        products_kernel,
        out_shape=jax.ShapeDtypeStruct((groups, size, size), jnp.bfloat16),
        grid_spec=pltpu.PrefetchScalarGridSpec(
            num_scalar_prefetch=1,
            grid=(count,),
            in_specs=[
                pl.BlockSpec((1, size, size), lambda g, t: (g // phys_count, 0, 0)),
                pl.BlockSpec((1, size, size), lambda g, t: (g, 0, 0)),
            ],
            out_specs=pl.BlockSpec((1, size, size), lambda g, t: (t[g], 0, 0)),
        ),
        compiler_params=pltpu.CompilerParams(vmem_limit_bytes=32 * 2**20),
    )(target, factor, blocks)


def eliminate(sectors):
    groups = TILE // SUB
    lane = lax.broadcasted_iota(jnp.int32, (SUB, TILE), 1)
    sub = lax.broadcasted_iota(jnp.int32, (SUB, TILE), 0)
    for q in range(groups):
        base = q * SUB
        spread = [
            {
                g: [
                    jnp.broadcast_to(rows[g][:, base + j : base + j + 1], (SUB, TILE))
                    for j in range(SUB)
                ]
                for g in range(q, groups)
            }
            for rows in sectors
        ]
        for j in range(SUB):
            here = lane == base + j
            below = sub > j
            for rows, columns in zip(sectors, spread):
                top = columns[q]
                inverse = 1.0 / jnp.broadcast_to(top[j][j : j + 1, :], (SUB, TILE))
                pivot_row = jnp.broadcast_to(rows[q][j : j + 1, :], (SUB, TILE))
                pivot_row = jnp.where(here, 1.0, pivot_row) * inverse
                ahead = [
                    jnp.broadcast_to(top[m][j : j + 1, :], (SUB, TILE)) * inverse
                    for m in range(j + 1, SUB)
                ]
                for g in range(q, groups):
                    column = columns[g][j]
                    clear = here
                    if g == q:
                        column = jnp.where(below, column, 0.0)
                        clear = here & below
                    rows[g] = jnp.where(clear, 0.0, rows[g]) - column * pivot_row
                    for m in range(j + 1, SUB):
                        columns[g][m] = columns[g][m] - column * ahead[m - j - 1]


def factor_kernel(last, phys_count, idx_ref, width_ref, recv_ref, *refs):
    if last:
        upper_ref, iso_ref, work, head, rest, lead, tail = refs
    else:
        upper_ref, work, head, rest = refs
    sec_local, size = work.shape[0], work.shape[1]
    steps = size // TILE

    def add_gram(t, _):
        b = t // phys_count
        x = recv_ref[idx_ref[t]]
        part = lax.dot_general(
            x, x, (((0,), (0,)), ((), ())), preferred_element_type=jnp.float32
        )

        @pl.when(t % phys_count == 0)
        def _():
            r = lax.broadcasted_iota(jnp.int32, (size, size), 0)
            c = lax.broadcasted_iota(jnp.int32, (size, size), 1)
            work[b] = part + jnp.where((r == c) & (c >= width_ref[b]), 1.0, 0.0)

        @pl.when(t % phys_count != 0)
        def _():
            work[b] = work[b] + part

        return 0

    lax.fori_loop(0, sec_local * phys_count, add_gram, 0)
    lane = lax.broadcasted_iota(jnp.int32, (SUB, TILE), 1)
    sub = lax.broadcasted_iota(jnp.int32, (SUB, TILE), 0)
    block_of_lane = lax.broadcasted_iota(jnp.int32, (TILE, size), 1) // TILE

    def step(k, _):
        at = pl.ds(pl.multiple_of(k * TILE, TILE), TILE)
        sectors = [
            [
                work[b, pl.ds(pl.multiple_of(k * TILE + SUB * g, SUB), SUB), at]
                for g in range(TILE // SUB)
            ]
            for b in range(sec_local)
        ]
        eliminate(sectors)
        for b in range(sec_local):
            for g in range(TILE // SUB):
                m = sectors[b][g]
                row = sub + SUB * g
                diag = jnp.sum(jnp.where(lane == row, m, 0.0), axis=1, keepdims=True)
                scale = jnp.broadcast_to(lax.rsqrt(diag), (SUB, TILE))
                at_g = pl.ds(SUB * g, SUB)
                head[b, at_g, :] = jnp.where(lane >= row, m, 0.0) * scale
                rest[b, at_g, :] = jnp.where(
                    lane < row, m, jnp.where(lane == row, 1.0, 0.0)
                ) * scale
        for b in range(sec_local):
            row = jnp.dot(
                rest[b], work[b, at, :], precision=HIGH, preferred_element_type=jnp.float32
            )
            work[b, at, :] = row
            work[b, at, at] = rest[b]
            upper_ref[b, at, :] = jnp.where(block_of_lane > k, row, 0.0).astype(upper_ref.dtype)
            upper_ref[b, at, at] = head[b].astype(upper_ref.dtype)
        for i in range(1, steps):

            @pl.when(i > k)
            def _():
                mine = pl.ds(i * TILE, TILE)
                for b in range(sec_local):
                    work[b, mine, at] = jnp.zeros((TILE, TILE), jnp.float32)
                    work[b, mine, :] = work[b, mine, :] - lax.dot_general(
                        work[b, at, mine],
                        work[b, at, :],
                        (((0,), (0,)), ((), ())),
                        precision=HIGH,
                        preferred_element_type=jnp.float32,
                    )

        return 0

    lax.fori_loop(0, steps, step, 0)
    if last:
        scale = math.sqrt(phys_count * size)
        for b in range(sec_local):
            for i in range(steps):
                mine = pl.ds(i * TILE, TILE)
                w = jnp.where(block_of_lane <= i, work[b, mine, :], 0.0) * scale
                hi = w.astype(jnp.bfloat16)
                lead[b, mine, :] = hi
                tail[b, mine, :] = (w - hi.astype(jnp.float32)).astype(jnp.bfloat16)

        def apply(t, _):
            b = t // phys_count
            x = recv_ref[idx_ref[t]]
            dims = (((1,), (1,)), ((), ()))
            iso_ref[t] = lax.dot_general(
                x, lead[b], dims, preferred_element_type=jnp.float32
            ) + lax.dot_general(x, tail[b], dims, preferred_element_type=jnp.float32)
            return 0

        lax.fori_loop(0, sec_local * phys_count, apply, 0)


def factorise(received, index, widths, sec_local, phys_count, last):
    size = received.shape[-1]
    vmem = pl.BlockSpec(memory_space=pltpu.VMEM)
    smem = pl.BlockSpec(memory_space=pltpu.SMEM)
    full = (sec_local, size, size)
    out_shape = [jax.ShapeDtypeStruct(full, jnp.float32 if last else jnp.bfloat16)]
    scratch = [
        pltpu.VMEM(full, jnp.float32),
        pltpu.VMEM((sec_local, TILE, TILE), jnp.float32),
        pltpu.VMEM((sec_local, TILE, TILE), jnp.float32),
    ]
    if last:
        out_shape.append(
            jax.ShapeDtypeStruct((sec_local * phys_count, size, size), jnp.float32)
        )
        scratch += [pltpu.VMEM(full, jnp.bfloat16)] * 2
    return pl.pallas_call(
        functools.partial(factor_kernel, last, phys_count),
        out_shape=out_shape,
        in_specs=[smem, smem, vmem],
        out_specs=[vmem] * len(out_shape),
        scratch_shapes=scratch,
        compiler_params=pltpu.CompilerParams(vmem_limit_bytes=48 * 2**20),
    )(index, widths, received)


def body(tensors, factors, sector_sizes, merging):
    site_index = lax.axis_index("site")
    sec_index = lax.axis_index("sec")
    site_count = lax.axis_size("site")
    sec_groups = lax.axis_size("sec")
    blocks = tensors[0]
    sec_local, phys_count, size = (blocks.shape[0], blocks.shape[1], blocks.shape[3])
    local_count = sec_local * phys_count
    blocks = blocks.reshape(local_count, size, size)
    rows = lax.dynamic_index_in_dim(merging, site_index, 0, keepdims=False)
    next_widths = lax.dynamic_index_in_dim(
        sector_sizes, (site_index + 1) % site_count, 0, keepdims=False
    )
    widths = lax.dynamic_slice_in_dim(next_widths, sec_index * sec_local, sec_local)
    own = lax.dynamic_slice_in_dim(rows, sec_index * sec_local, sec_local)
    target = own.reshape(local_count) // sec_local
    wanted = sec_index * sec_local + jnp.arange(sec_local, dtype=jnp.int32)
    match = (rows[None] == wanted[:, None, None]).astype(jnp.int32)
    left = jnp.arange(rows.shape[0], dtype=jnp.int32) // sec_local
    index = jnp.sum(match * left[None, :, None], axis=1).reshape(local_count)
    carried = factors[0]
    for step_index in range(ROUNDS):
        last = step_index + 1 == ROUNDS
        outgoing = products_by_target(carried, blocks, target, sec_groups)
        received = lax.all_to_all(outgoing, "sec", split_axis=0, concat_axis=0, tiled=True)
        out = factorise(received, index, widths, sec_local, phys_count, last)
        if not last:
            carried = from_behind(out[0], "site", 1)
    upper, isometry = out
    return (isometry.reshape(1, sec_local, phys_count, size, size), upper[None])


def solution(mesh):
    in_specs = (P("site", "sec", None, None, None), P("site", "sec", None, None), P(), P())
    out_specs = (P("site", "sec", None, None, None), P("site", "sec", None, None))
    return jax.shard_map(body, mesh=mesh, in_specs=in_specs, out_specs=out_specs, check_vma=False)
```

```python
import functools
import math

import jax
import jax.numpy as jnp
from jax import lax
from jax.experimental import pallas as pl
from jax.experimental.pallas import tpu as pltpu
from jax.sharding import PartitionSpec as P

ROUNDS = 3
TILE = 128
SUB = 8
HIGH = lax.Precision.HIGHEST


def from_behind(shard, axis, by):
    size = lax.axis_size(axis)
    return lax.ppermute(shard, axis, [(i, (i + by) % size) for i in range(size)])


def products_kernel(target_ref, factor_ref, block_ref, out_ref):
    out_ref[0] = jnp.dot(
        factor_ref[0].astype(jnp.bfloat16), block_ref[0], preferred_element_type=jnp.float32
    ).astype(jnp.bfloat16)


def products_by_target(factor, blocks, target, groups, row, phys_count):
    count, size = blocks.shape[0], blocks.shape[-1]
    height, depth = factor.shape[1:]
    return pl.pallas_call(
        products_kernel,
        out_shape=jax.ShapeDtypeStruct((groups, height, size), jnp.bfloat16),
        grid_spec=pltpu.PrefetchScalarGridSpec(
            num_scalar_prefetch=1,
            grid=(count,),
            in_specs=[
                pl.BlockSpec((1, height, depth), lambda g, t: (g // phys_count, 0, 0)),
                pl.BlockSpec((1, depth, size), lambda g, t: (g, row, 0)),
            ],
            out_specs=pl.BlockSpec((1, height, size), lambda g, t: (t[g], 0, 0)),
        ),
        compiler_params=pltpu.CompilerParams(vmem_limit_bytes=32 * 2**20),
    )(target, factor, blocks)


def eliminate(sectors):
    groups = TILE // SUB
    lane = lax.broadcasted_iota(jnp.int32, (SUB, TILE), 1)
    sub = lax.broadcasted_iota(jnp.int32, (SUB, TILE), 0)
    for q in range(groups):
        base = q * SUB
        spread = [
            {
                g: [
                    jnp.broadcast_to(rows[g][:, base + j : base + j + 1], (SUB, TILE))
                    for j in range(SUB)
                ]
                for g in range(q, groups)
            }
            for rows in sectors
        ]
        for j in range(SUB):
            here = lane == base + j
            below = sub > j
            for rows, columns in zip(sectors, spread):
                top = columns[q]
                inverse = 1.0 / jnp.broadcast_to(top[j][j : j + 1, :], (SUB, TILE))
                pivot_row = jnp.broadcast_to(rows[q][j : j + 1, :], (SUB, TILE))
                pivot_row = jnp.where(here, 1.0, pivot_row) * inverse
                ahead = [
                    jnp.broadcast_to(top[m][j : j + 1, :], (SUB, TILE)) * inverse
                    for m in range(j + 1, SUB)
                ]
                for g in range(q, groups):
                    column = columns[g][j]
                    clear = here
                    if g == q:
                        column = jnp.where(below, column, 0.0)
                        clear = here & below
                    rows[g] = jnp.where(clear, 0.0, rows[g]) - column * pivot_row
                    for m in range(j + 1, SUB):
                        columns[g][m] = columns[g][m] - column * ahead[m - j - 1]


def transposed_dot(x, y, precision=None):
    return lax.dot_general(
        x, y, (((0,), (0,)), ((), ())), precision=precision, preferred_element_type=jnp.float32
    )


def factor_blocks(work, head, rest, upper_ref, inverse_ref):
    sec_local, size = work.shape[0], work.shape[1]
    steps = size // TILE
    lane = lax.broadcasted_iota(jnp.int32, (SUB, TILE), 1)
    sub = lax.broadcasted_iota(jnp.int32, (SUB, TILE), 0)
    block_of_lane = lax.broadcasted_iota(jnp.int32, (TILE, size), 1) // TILE

    def step(k, _):
        at = pl.ds(pl.multiple_of(k * TILE, TILE), TILE)
        sectors = [
            [
                work[b, pl.ds(pl.multiple_of(k * TILE + SUB * g, SUB), SUB), at]
                for g in range(TILE // SUB)
            ]
            for b in range(sec_local)
        ]
        eliminate(sectors)
        for b in range(sec_local):
            for g in range(TILE // SUB):
                m = sectors[b][g]
                row = sub + SUB * g
                diag = jnp.sum(jnp.where(lane == row, m, 0.0), axis=1, keepdims=True)
                scale = jnp.broadcast_to(lax.rsqrt(diag), (SUB, TILE))
                at_g = pl.ds(SUB * g, SUB)
                head[b, at_g, :] = jnp.where(lane >= row, m, 0.0) * scale
                rest[b, at_g, :] = (
                    jnp.where(lane < row, m, jnp.where(lane == row, 1.0, 0.0)) * scale
                )
        for b in range(sec_local):
            row = jnp.dot(
                rest[b], work[b, at, :], precision=HIGH, preferred_element_type=jnp.float32
            )
            work[b, at, :] = row
            work[b, at, at] = rest[b]
            upper_ref[b, at, :] = jnp.where(block_of_lane > k, row, 0.0).astype(upper_ref.dtype)
            upper_ref[b, at, at] = head[b].astype(upper_ref.dtype)
        for i in range(1, steps):

            @pl.when(i > k)
            def _():
                mine = pl.ds(i * TILE, TILE)
                for b in range(sec_local):
                    work[b, mine, at] = jnp.zeros((TILE, TILE), jnp.float32)
                    work[b, mine, :] = work[b, mine, :] - transposed_dot(
                        work[b, at, mine], work[b, at, :], HIGH
                    )

        return 0

    lax.fori_loop(0, steps, step, 0)
    for b in range(sec_local):
        for i in range(steps):
            mine = pl.ds(i * TILE, TILE)
            inverse_ref[b, mine, :] = jnp.where(block_of_lane <= i, work[b, mine, :], 0.0)


def padded(size, start, width):
    r = lax.broadcasted_iota(jnp.int32, (size, size), 0)
    c = lax.broadcasted_iota(jnp.int32, (size, size), 1)
    return jnp.where((r == c) & (c + start >= width), 1.0, 0.0)


def first_kernel(phys_count, idx_ref, width_ref, top_ref, low_ref, upper_ref, inverse_ref, work, head, rest):
    sec_local, half = work.shape[0], work.shape[1]
    for b in range(sec_local):
        work[b] = padded(half, 0, width_ref[b])

    def add_gram(t, _):
        b = t // phys_count
        x = top_ref[idx_ref[t], :, :half]
        y = low_ref[idx_ref[t]]
        work[b] = work[b] + transposed_dot(x, x) + transposed_dot(y, y)
        return 0

    lax.fori_loop(0, sec_local * phys_count, add_gram, 0)
    factor_blocks(work, head, rest, upper_ref, inverse_ref)


def middle_kernel(
    phys_count, idx_ref, width_ref, top_ref, low_ref, high_ref, upper_ref, inverse_ref,
    strip_ref, remain_ref, cross,
):
    sec_local, half = cross.shape[0], cross.shape[1]
    for b in range(sec_local):
        cross[b] = jnp.zeros_like(cross[b])
        remain_ref[b] = padded(half, half, width_ref[b])

    def add_gram(t, _):
        b = t // phys_count
        x = top_ref[idx_ref[t], :, :half]
        y = top_ref[idx_ref[t], :, half:]
        u = low_ref[idx_ref[t]]
        v = high_ref[idx_ref[t]]
        cross[b] = cross[b] + transposed_dot(x, y) + transposed_dot(u, v)
        remain_ref[b] = remain_ref[b] + transposed_dot(y, y) + transposed_dot(v, v)
        return 0

    lax.fori_loop(0, sec_local * phys_count, add_gram, 0)
    for b in range(sec_local):
        row = jnp.dot(
            inverse_ref[b], cross[b], precision=HIGH, preferred_element_type=jnp.float32
        )
        remain_ref[b] = remain_ref[b] - transposed_dot(row, row, HIGH)
        strip_ref[b, :, :half] = upper_ref[b].astype(strip_ref.dtype)
        strip_ref[b, :, half:] = row.astype(strip_ref.dtype)


def second_kernel(remain_ref, upper_ref, inverse_ref, work, head, rest):
    work[...] = remain_ref[...]
    factor_blocks(work, head, rest, upper_ref, inverse_ref)


def isometry_kernel(
    phys_count, idx_ref, top_ref, low_ref, high_ref, strip_ref, first_ref, second_ref, iso_ref,
    lead, tail,
):
    sec_local, half = first_ref.shape[0], first_ref.shape[1]
    scale = math.sqrt(phys_count * 2 * half)

    def split(b, rows, columns, value):
        value = value * scale
        hi = value.astype(jnp.bfloat16)
        lead[b, rows, columns] = hi
        tail[b, rows, columns] = (value - hi.astype(jnp.float32)).astype(jnp.bfloat16)

    one, two = pl.ds(0, half), pl.ds(half, half)
    for b in range(sec_local):
        mixed = transposed_dot(strip_ref[b, :, half:], first_ref[b], HIGH)
        mixed = -jnp.dot(
            second_ref[b], mixed, precision=HIGH, preferred_element_type=jnp.float32
        )
        split(b, one, one, first_ref[b])
        split(b, one, two, jnp.zeros((half, half), jnp.float32))
        split(b, two, one, mixed)
        split(b, two, two, second_ref[b])

    def across(x, w):
        return lax.dot_general(
            x, w, (((1,), (1,)), ((), ())), preferred_element_type=jnp.float32
        )

    def apply(t, _):
        b = t // phys_count
        for rows, left, right in (
            (one, top_ref[idx_ref[t], :, :half], top_ref[idx_ref[t], :, half:]),
            (two, low_ref[idx_ref[t]], high_ref[idx_ref[t]]),
        ):
            iso_ref[t, rows, one] = across(left, lead[b, one, one]) + across(
                left, tail[b, one, one]
            )
            iso_ref[t, rows, two] = (
                across(left, lead[b, two, one])
                + across(left, tail[b, two, one])
                + across(right, lead[b, two, two])
                + across(right, tail[b, two, two])
            )
        return 0

    lax.fori_loop(0, sec_local * phys_count, apply, 0)


def local_call(kernel, outs, scratch, scalars, arrays, flops):
    vmem = pl.BlockSpec(memory_space=pltpu.VMEM)
    smem = pl.BlockSpec(memory_space=pltpu.SMEM)
    return pl.pallas_call(
        kernel,
        out_shape=[jax.ShapeDtypeStruct(shape, dtype) for shape, dtype in outs],
        in_specs=[smem] * len(scalars) + [vmem] * len(arrays),
        out_specs=[vmem] * len(outs),
        scratch_shapes=[pltpu.VMEM(shape, dtype) for shape, dtype in scratch],
        compiler_params=pltpu.CompilerParams(vmem_limit_bytes=48 * 2**20),
        cost_estimate=pl.CostEstimate(flops=flops, bytes_accessed=2**20, transcendentals=0),
    )(*scalars, *arrays)


def route(outgoing):
    return lax.all_to_all(outgoing, "sec", split_axis=0, concat_axis=0, tiled=True)


def factor_round(strip, corner, blocks, target, index, widths, top, phys_count, groups, last):
    sec_local, half = corner.shape[0], corner.shape[1]
    square = ((sec_local, half, half), jnp.float32)
    tiles = [((sec_local, TILE, TILE), jnp.float32)] * 2
    kind = jnp.float32 if last else jnp.bfloat16
    outgoing = products_by_target(corner, blocks, target, groups, 1, phys_count)
    outgoing, top = lax.optimization_barrier((outgoing, top))
    low = route(outgoing[:, :, :half])
    low, outgoing = lax.optimization_barrier((low, outgoing[:, :, half:]))
    high = route(outgoing)
    upper, inverse = local_call(
        functools.partial(first_kernel, phys_count),
        [square, square],
        [square] + tiles,
        [index, widths],
        [top, low],
        2 * 10**10,
    )
    high, upper, inverse = lax.optimization_barrier((high, upper, inverse))
    strip, remain = local_call(
        functools.partial(middle_kernel, phys_count),
        [((sec_local, half, 2 * half), kind), square],
        [square],
        [index, widths],
        [top, low, high, upper, inverse],
        2 * 10**9,
    )
    next_top = None
    if not last:
        carried = from_behind(strip, "site", 1)
        sent = products_by_target(carried, blocks, target, groups, 0, phys_count)
        sent, remain = lax.optimization_barrier((sent, remain))
        next_top = route(sent)
    corner, inverse_two = local_call(
        second_kernel,
        [((sec_local, half, half), kind), square],
        [square] + tiles,
        [],
        [remain],
        2 * 10**10,
    )
    if not last:
        return strip, from_behind(corner, "site", 1), next_top
    full = ((sec_local, 2 * half, 2 * half), jnp.bfloat16)
    (isometry,) = local_call(
        functools.partial(isometry_kernel, phys_count),
        [((sec_local * phys_count, 2 * half, 2 * half), jnp.float32)],
        [full, full],
        [index],
        [top, low, high, strip, inverse, inverse_two],
        4 * 10**9,
    )
    bottom = jnp.pad(corner, ((0, 0), (0, 0), (half, 0)))
    return jnp.concatenate([strip, bottom], axis=1), isometry


def body(tensors, factors, sector_sizes, merging):
    site_index = lax.axis_index("site")
    sec_index = lax.axis_index("sec")
    site_count = lax.axis_size("site")
    sec_groups = lax.axis_size("sec")
    blocks = tensors[0]
    sec_local, phys_count, size = (blocks.shape[0], blocks.shape[1], blocks.shape[3])
    local_count = sec_local * phys_count
    blocks = blocks.reshape(local_count, size, size)
    rows = lax.dynamic_index_in_dim(merging, site_index, 0, keepdims=False)
    next_widths = lax.dynamic_index_in_dim(
        sector_sizes, (site_index + 1) % site_count, 0, keepdims=False
    )
    widths = lax.dynamic_slice_in_dim(next_widths, sec_index * sec_local, sec_local)
    own = lax.dynamic_slice_in_dim(rows, sec_index * sec_local, sec_local)
    target = own.reshape(local_count) // sec_local
    wanted = sec_index * sec_local + jnp.arange(sec_local, dtype=jnp.int32)
    match = (rows[None] == wanted[:, None, None]).astype(jnp.int32)
    left = jnp.arange(rows.shape[0], dtype=jnp.int32) // sec_local
    index = jnp.sum(match * left[None, :, None], axis=1).reshape(local_count)
    half = size // 2
    strip, corner = factors[0, :, :half], factors[0, :, half:, half:]
    top = route(products_by_target(strip, blocks, target, sec_groups, 0, phys_count))
    for step_index in range(ROUNDS):
        last = step_index + 1 == ROUNDS
        out = factor_round(
            strip, corner, blocks, target, index, widths, top, phys_count, sec_groups, last
        )
        if not last:
            strip, corner, top = out
    upper, isometry = out
    return (isometry.reshape(1, sec_local, phys_count, size, size), upper[None])


def solution(mesh):
    in_specs = (P("site", "sec", None, None, None), P("site", "sec", None, None), P(), P())
    out_specs = (P("site", "sec", None, None, None), P("site", "sec", None, None))
    return jax.shard_map(body, mesh=mesh, in_specs=in_specs, out_specs=out_specs, check_vma=False)
```
